32 devices in a mesh: src: 4 (over y, x), tgt: 4 (over z), rep: 2 (over core).
Axes of the slice: x: 2, y: 2, z: 4, core: 2. Of those that a mesh axis runs over, the one named last changes fastest.
Arguments:
- omega: bfloat16 [128, 32768], P('rep', 'src'), may hold values from -6 to 6
- leaf: bfloat16 [4, 64, 32768], P('tgt', None, 'src'), may hold values from -0.0625 to 0.0625
- factors: bfloat16 [4, 4, 2, 64, 128], P('tgt', 'src'), may hold values from -0.5 to 0.5
- pattern: int32 [4, 4, 2, 2, 4], P('tgt', 'src'), may hold values 0 or 1
- ranks: int32 [2], replicated, may hold values from 32 to 64
- outer: bfloat16 [64, 8192], P(None, ('tgt', 'src')), may hold values from -0.375 to 0.375
Outputs:
- samples: float32 [128, 8192], P('rep', ('tgt', 'src'))
The draws below stay inside these ranges and needn't reach their ends.
All inputs are finite; a program needn't handle non-finite values. No bound on the sum of `pattern` on one device may be relied on, other than what follows from the above.
Results may differ from the reference program's by a relative error of at most 0.02.
Values may be sent and summed in bfloat16 or wider, within the bound.
A program may use at most 64 MiB of HBM per device.

```python
import jax
import jax.numpy as jnp
from jax import lax

K = 64
R_ALL = 128
BLK = 32
LEVELS = 2
NS_ITERS = 3
PTS = 8192
NS = 32768
TPB = 2048
NO = 8192
N_SRC = 4
N_TGT = 4


def touch_ends(values, rng, least, largest):
    index_at = [jax.random.randint(jax.random.fold_in(rng, axis), (), 0, length) for axis, length in enumerate(values.shape)]
    main_axis = values.shape.index(max(values.shape))
    beside = index_at[:main_axis] + [(index_at[main_axis] + 1) % values.shape[main_axis]] + index_at[main_axis + 1:]
    return values.at[tuple(index_at)].set(least).at[tuple(beside)].set(largest)


def block_levels(key, shape, shards, smallest, top_value):
    level, own = 1.0, jax.random.fold_in(key, 6)
    for dim, shards_of in shards:
        steps = jnp.exp(jax.random.uniform(jax.random.fold_in(own, dim), (shards_of,), jnp.float32, smallest / len(shards), top_value / len(shards)))
        level = level * jnp.repeat(steps, shape[dim] // shards_of).reshape([-1 if axis == dim else 1 for axis in range(len(shape))])
    return level


def noise(own_key, shape, deviation, limit, pieces=(), kind=jnp.bfloat16):
    entries = deviation * jax.random.normal(own_key, shape, jnp.float32)
    if pieces:
        entries = entries * block_levels(own_key, shape, pieces, -0.22, 0.18)
    return jnp.clip(entries, -limit, limit).astype(kind)


def setup_inputs(seed: int = 0) -> dict:
    key_of = jax.random.split(jax.random.key(seed), 7)
    omega = noise(key_of[0], (R_ALL, NS), 1.0, 6.0, ((0, 2), (1, 4)))
    leaf = noise(key_of[1], (N_TGT, K, NS), PTS ** -0.5, 0.0625, ((0, 4), (2, 4)))
    factors = noise(key_of[2], (N_TGT, N_SRC, LEVELS, K, 2 * K), (2 * K) ** -0.5, 0.5, ((0, 4), (1, 4)))
    pattern = touch_ends((jax.random.randint(key_of[3], (N_TGT, N_SRC, LEVELS, K // BLK, 2 * K // BLK), 0, 4) < 3).astype(jnp.int32), jax.random.fold_in(key_of[3], 1), 0, 1)
    ranks = jax.random.randint(key_of[4], (LEVELS,), 32, 65).astype(jnp.int32)
    outer = noise(key_of[5], (K, NO), (K * N_SRC) ** -0.5, 0.375, ((1, 16),))
    return dict(omega=omega, leaf=leaf, factors=factors, pattern=pattern, ranks=ranks, outer=outer)


def polar_iteration(gram):
    scale = jnp.sqrt(lax.optimization_barrier(jnp.sum(gram * gram, axis=(-2, -1), keepdims=True))) + 1e-06
    upper = gram / scale
    eye = jnp.eye(K, dtype=jnp.float32)
    lower = jnp.broadcast_to(eye, gram.shape)
    for step in range(NS_ITERS):
        central_factor = 1.5 * eye - 0.5 * jnp.einsum('tsij,tsjk->tsik', lower, upper, precision=lax.Precision.HIGHEST)
        upper = jnp.einsum('tsij,tsjk->tsik', upper, central_factor, precision=lax.Precision.HIGHEST)
        lower = jnp.einsum('tsij,tsjk->tsik', central_factor, lower, precision=lax.Precision.HIGHEST)
    return (lower, scale)

def reference(omega, leaf, factors, pattern, ranks, outer):
    om_blocks = omega.reshape(R_ALL, N_SRC, PTS).astype(jnp.float32)

    def leaf_segment(leaf_t):
        blocks = leaf_t.reshape(K, N_SRC, PTS).astype(jnp.float32)
        return jnp.einsum('ksp,rsp->skr', blocks, om_blocks)
    piece = lax.map(leaf_segment, leaf).astype(jnp.bfloat16)
    sources = jnp.arange(N_SRC)
    rows = jnp.arange(K)
    for level in range(LEVELS):
        partner = piece[:, sources ^ 1 << level]
        lowside = (sources >> level & 1 == 0)[None, :, None, None]
        stacked = jnp.where(lowside, jnp.concatenate([piece, partner], 2), jnp.concatenate([partner, piece], 2))
        blocks = jnp.repeat(jnp.repeat(pattern[:, :, level], BLK, 2), BLK, 3)
        masked = factors[:, :, level] * blocks.astype(jnp.bfloat16)
        fresh = jnp.einsum('tsij,tsjr->tsir', masked.astype(jnp.float32), stacked.astype(jnp.float32)).astype(jnp.bfloat16)
        fresh32 = fresh.astype(jnp.float32)
        gram = jnp.einsum('tsir,tsjr->tsij', fresh32, fresh32, precision=lax.Precision.HIGHEST)
        lower, scale = polar_iteration(gram)
        whitened = jnp.einsum('tsij,tsjr->tsir', lower, fresh32, precision=lax.Precision.HIGHEST)
        whitened = whitened * jnp.sqrt(R_ALL / scale)
        keep = (rows < ranks[level])[None, None, :, None]
        piece = jnp.where(keep, whitened, 0.0).astype(jnp.bfloat16)
    reduced_sum = lax.optimization_barrier(jnp.sum(piece.astype(jnp.float32), axis=1))
    basis_matrices = outer.reshape(K, N_TGT, TPB).astype(jnp.float32)
    grand_total = jnp.einsum('jmg,mju->umg', basis_matrices, reduced_sum, precision=lax.Precision.HIGHEST)
    return grand_total.reshape(R_ALL, NO)
```

```python
import jax
import jax.numpy as jnp
from jax import lax
from jax.experimental import pallas as pl
from jax.experimental.pallas import tpu as pltpu
from jax.sharding import PartitionSpec as P

K = 64
R_ALL = 128
BLK = 32
LEVELS = 2
GROUP = 4
CHUNKS = 4
MESH = pl.DeviceIdType.MESH

F32 = jnp.float32
BF16 = jnp.bfloat16


def product(left, right, dims=((1,), (0,))):
    return lax.dot_general(
        left.astype(BF16), right.astype(BF16), (dims, ((), ())), preferred_element_type=F32
    )


def level_slot(level, source):
    if level == 0:
        return source
    return source // 2 + 2 * (source % 2)


def whiten(fresh_bf, own):
    eye = (
        lax.broadcasted_iota(jnp.int32, (K, K), 0) == lax.broadcasted_iota(jnp.int32, (K, K), 1)
    ).astype(F32)
    count = len(fresh_bf)
    each = range(count)
    gram = [product(f, f, ((1,), (1,))) for f in fresh_bf]
    squared = [product(g, g) for g in gram]
    norm = [jnp.sum(jnp.sum(g * g, axis=1, keepdims=True), axis=0, keepdims=True) for g in gram]
    scale = [jnp.sqrt(n) + 1e-06 for n in norm]
    inv = [1.0 / s for s in scale]
    gain = [jnp.sqrt(R_ALL * i) for i in inv]
    a = [g * i for g, i in zip(gram, inv)]
    t = [s * i * i for s, i in zip(squared, inv)]
    target = [f[:, :K] if own else f for f in fresh_bf]
    w = [1.5 * target[i].astype(F32) - 0.5 * product(a[i], target[i]) for i in each]
    p = [2.25 * a[i] - 1.5 * t[i] + 0.25 * product(t[i], a[i]) for i in each]
    q = [product(p[i], p[i]) for i in each]
    w = [1.5 * w[i] - 0.5 * product(p[i], w[i]) for i in each]
    p = [2.25 * p[i] - 1.5 * q[i] + 0.25 * product(q[i], p[i]) for i in each]
    w = [1.5 * w[i] - 0.5 * product(p[i], w[i]) for i in each]
    return [w[i] * gain[i] for i in each]


def kernel(
    omega_hbm, leaf_hbm, factors_hbm, pattern_hbm, ranks_hbm, outer_hbm, out_ref,
    omega, leaf, factors, pattern, ranks, outer, masked, gathered,
    load_sem, chunk_sem, fsend, frecv, psend, precv, *, finish,
):
    src = lax.axis_index("src")
    tgt = lax.axis_index("tgt")
    rep = lax.axis_index("rep")
    base = src - lax.rem(src, GROUP)
    me = src - base

    def peer(step, other):
        return (base + lax.rem(me + step, GROUP), tgt, lax.rem(rep + other, 2))

    peers = [(step, other) for other in (0, 1) for step in range(GROUP) if (step, other) != (0, 0)]
    barrier = pltpu.get_barrier_semaphore()
    for step, other in peers:
        pl.semaphore_signal(barrier, inc=1, device_id=peer(step, other), device_id_type=MESH)

    small = [
        pltpu.make_async_copy(a, b, load_sem.at[i])
        for i, (a, b) in enumerate(
            (
                (pattern_hbm, pattern),
                (factors_hbm.at[0, 0], factors),
                (ranks_hbm, ranks),
            )
        )
    ]
    load_outer = pltpu.make_async_copy(outer_hbm, outer, load_sem.at[3])
    for copy in small:
        copy.start()
    width = omega.shape[1] // CHUNKS
    big = []
    for c in range(CHUNKS):
        cols = pl.ds(c * width, width)
        pair = (
            pltpu.make_async_copy(omega_hbm.at[:, cols], omega.at[:, cols], chunk_sem.at[0, c]),
            pltpu.make_async_copy(leaf_hbm.at[0, :, cols], leaf.at[:, cols], chunk_sem.at[1, c]),
        )
        for copy in pair:
            copy.start()
        big.append(pair)
    load_outer.start()

    for copy in small:
        copy.wait()
    lane = lax.broadcasted_iota(jnp.int32, (1, 2 * K), 1) // BLK
    for level in range(LEVELS):
        at = pl.multiple_of(level_slot(level, me) * K, K)
        for i in range(K // BLK):
            keep = jnp.zeros((1, 2 * K), F32)
            for j in range(2 * K // BLK):
                keep = jnp.where(lane == j, pattern[0, 0, level, i, j].astype(F32), keep)
            block = factors[level, i * BLK:(i + 1) * BLK, :].astype(F32) * keep
            masked[level, pl.ds(at + i * BLK, BLK), :] = block.astype(BF16)

    pl.semaphore_wait(barrier, len(peers))
    fcopies = []
    for level in range(LEVELS):
        at = pl.multiple_of(level_slot(level, me) * K, K)
        rows = masked.at[level, pl.ds(at, K), :]
        for step in range(1, GROUP):
            copy = pltpu.make_async_remote_copy(
                src_ref=rows, dst_ref=rows,
                send_sem=fsend.at[level, step], recv_sem=frecv.at[level, step],
                device_id=peer(step, 0), device_id_type=MESH,
            )
            copy.start()
            fcopies.append(copy)

    piece = jnp.zeros((K, K), F32)
    for c in range(CHUNKS):
        for copy in big[c]:
            copy.wait()
        cols = slice(c * width, (c + 1) * width)
        piece = piece + product(leaf[:, cols], omega[:, cols], ((1,), (1,)))
    at = pl.multiple_of(me * K, K)
    gathered[0, pl.ds(at, K), :] = piece.astype(BF16)
    pcopies = []
    for step, other in peers:
        copy = pltpu.make_async_remote_copy(
            src_ref=gathered.at[0, pl.ds(at, K), :],
            dst_ref=gathered.at[other, pl.ds(at, K), :],
            send_sem=psend.at[other, step], recv_sem=precv.at[other, step],
            device_id=peer(step, other), device_id_type=MESH,
        )
        copy.start()
        pcopies.append(copy)

    for copy in fcopies:
        copy.wait_recv()
    for copy in pcopies:
        copy.wait_recv()

    row = lax.broadcasted_iota(jnp.int32, (K, 1), 0)
    stacks = [
        jnp.concatenate([gathered[0, h * 2 * K:(h + 1) * 2 * K, :],
                         gathered[1, h * 2 * K:(h + 1) * 2 * K, :]], axis=1)
        for h in range(2)
    ]
    order = (0, 1, 2, 3)
    for level in range(LEVELS):
        fresh = []
        for h in range(2):
            both = product(masked[level, h * 2 * K:(h + 1) * 2 * K, :], stacks[h]).astype(BF16)
            fresh += [both[:K], both[K:]]
        pieces = whiten(fresh, level == LEVELS - 1)
        pieces = [jnp.where(row < ranks[level], x, 0.0).astype(BF16) for x in pieces]
        if level == 0:
            stacks = [
                jnp.concatenate([pieces[0], pieces[2]], axis=0),
                jnp.concatenate([pieces[1], pieces[3]], axis=0),
            ]
    total = (pieces[0].astype(F32) + pieces[1].astype(F32)) + (
        pieces[2].astype(F32) + pieces[3].astype(F32)
    )
    load_outer.wait()
    if finish:
        out_ref[...] = product(total, outer[...], ((0,), (0,)))
    else:
        out_ref[...] = total
    for copy in fcopies:
        copy.wait_send()
    for copy in pcopies:
        copy.wait_send()


def shards(omega, leaf, factors, pattern, ranks, outer):
    groups = lax.axis_size("src") // GROUP
    finish = groups == 1
    shape = (K, outer.shape[1]) if finish else (K, K)
    hbm = pl.BlockSpec(memory_space=pl.ANY)
    result = pl.pallas_call(
        lambda *refs: kernel(*refs, finish=finish),
        out_shape=jax.ShapeDtypeStruct(shape, F32),
        in_specs=[hbm] * 6,
        out_specs=pl.BlockSpec(memory_space=pltpu.VMEM),
        scratch_shapes=[
            pltpu.VMEM(omega.shape, BF16),
            pltpu.VMEM(leaf.shape[1:], BF16),
            pltpu.VMEM((LEVELS, K, 2 * K), BF16),
            pltpu.SMEM(pattern.shape, jnp.int32),
            pltpu.SMEM((LEVELS,), jnp.int32),
            pltpu.VMEM(outer.shape, BF16),
            pltpu.VMEM((LEVELS, GROUP * K, 2 * K), BF16),
            pltpu.VMEM((2, GROUP * K, K), BF16),
            pltpu.SemaphoreType.DMA((4,)),
            pltpu.SemaphoreType.DMA((2, CHUNKS)),
            pltpu.SemaphoreType.DMA((LEVELS, GROUP)),
            pltpu.SemaphoreType.DMA((LEVELS, GROUP)),
            pltpu.SemaphoreType.DMA((2, GROUP)),
            pltpu.SemaphoreType.DMA((2, GROUP)),
        ],
        compiler_params=pltpu.CompilerParams(
            collective_id=0, has_side_effects=True, vmem_limit_bytes=32 * 1024 * 1024
        ),
        cost_estimate=pl.CostEstimate(
            flops=2 * K * K * omega.shape[1], bytes_accessed=2 * omega.size * 2, transcendentals=0
        ),
    )(omega, leaf, factors, pattern, ranks, outer)
    if finish:
        return result
    total = lax.psum(result, "src") * (1.0 / GROUP)
    return lax.dot_general(
        total, outer.astype(F32), (((0,), (0,)), ((), ())), precision=lax.Precision.HIGHEST
    )


def solution(mesh):
    return jax.shard_map(
        shards,
        mesh=mesh,
        in_specs=(
            P("rep", "src"),
            P("tgt", None, "src"),
            P("tgt", "src", None, None, None),
            P("tgt", "src", None, None, None),
            P(),
            P(None, ("tgt", "src")),
        ),
        out_specs=P("rep", ("tgt", "src")),
        check_vma=False,
    )
```

```python
import jax
import jax.numpy as jnp
from jax import lax
from jax.experimental import pallas as pl
from jax.experimental.pallas import tpu as pltpu
from jax.sharding import PartitionSpec as P

K = 64
R_ALL = 128
BLK = 32
LEVELS = 2
GROUP = 4
CHUNKS = 4
MESH = pl.DeviceIdType.MESH

F32 = jnp.float32
BF16 = jnp.bfloat16


def product(left, right, dims=((1,), (0,))):
    return lax.dot_general(
        left.astype(BF16), right.astype(BF16), (dims, ((), ())), preferred_element_type=F32
    )


def level_slot(level, source):
    if level == 0:
        return source
    return source // 2 + 2 * (source % 2)


def whiten(fresh_bf, own):
    eye = (
        lax.broadcasted_iota(jnp.int32, (K, K), 0) == lax.broadcasted_iota(jnp.int32, (K, K), 1)
    ).astype(F32)
    count = len(fresh_bf)
    each = range(count)
    gram = [product(f, f, ((1,), (1,))) for f in fresh_bf]
    squared = [product(g, g) for g in gram]
    norm = [jnp.sum(jnp.sum(g * g, axis=1, keepdims=True), axis=0, keepdims=True) for g in gram]
    scale = [jnp.sqrt(n) + 1e-06 for n in norm]
    inv = [1.0 / s for s in scale]
    gain = [jnp.sqrt(R_ALL * i) for i in inv]
    a = [g * i for g, i in zip(gram, inv)]
    t = [s * i * i for s, i in zip(squared, inv)]
    target = [f[:, :K] if own else f for f in fresh_bf]
    w = [1.5 * target[i].astype(F32) - 0.5 * product(a[i], target[i]) for i in each]
    p = [2.25 * a[i] - 1.5 * t[i] + 0.25 * product(t[i], a[i]) for i in each]
    q = [product(p[i], p[i]) for i in each]
    w = [1.5 * w[i] - 0.5 * product(p[i], w[i]) for i in each]
    p = [2.25 * p[i] - 1.5 * q[i] + 0.25 * product(q[i], p[i]) for i in each]
    w = [1.5 * w[i] - 0.5 * product(p[i], w[i]) for i in each]
    return [w[i] * gain[i] for i in each]


def kernel(
    omega_hbm, leaf_hbm, factors_hbm, pattern_hbm, ranks_hbm, outer_hbm, out_ref,
    omega, leaf, factors, pattern, ranks, outer, masked, gathered,
    load_sem, chunk_sem, fsend, frecv, psend, precv, *, finish,
):
    src = lax.axis_index("src")
    tgt = lax.axis_index("tgt")
    rep = lax.axis_index("rep")
    base = src - lax.rem(src, GROUP)
    me = src - base

    def peer(step, other):
        high = lax.rem(me // 2 + step // 2, 2)
        low = lax.rem(lax.rem(me, 2) + step % 2, 2)
        return (base + 2 * high + low, tgt, lax.rem(rep + other, 2))

    peers = [(3, 0), (3, 1), (1, 0), (2, 0), (1, 1), (2, 1), (0, 1)]
    barrier = pltpu.get_barrier_semaphore()
    for step, other in peers:
        pl.semaphore_signal(barrier, inc=1, device_id=peer(step, other), device_id_type=MESH)

    small = [
        pltpu.make_async_copy(a, b, load_sem.at[i])
        for i, (a, b) in enumerate(
            (
                (pattern_hbm, pattern),
                (factors_hbm.at[0, 0], factors),
                (ranks_hbm, ranks),
            )
        )
    ]
    load_outer = pltpu.make_async_copy(outer_hbm, outer, load_sem.at[3])
    for copy in small:
        copy.start()
    width = omega.shape[1] // CHUNKS
    big = []
    for c in range(CHUNKS):
        cols = pl.ds(c * width, width)
        pair = (
            pltpu.make_async_copy(omega_hbm.at[:, cols], omega.at[:, cols], chunk_sem.at[0, c]),
            pltpu.make_async_copy(leaf_hbm.at[0, :, cols], leaf.at[:, cols], chunk_sem.at[1, c]),
        )
        for copy in pair:
            copy.start()
        big.append(pair)
    load_outer.start()

    for copy in small:
        copy.wait()
    lane = lax.broadcasted_iota(jnp.int32, (1, 2 * K), 1) // BLK
    for level in range(LEVELS):
        at = pl.multiple_of(level_slot(level, me) * K, K)
        for i in range(K // BLK):
            keep = jnp.zeros((1, 2 * K), F32)
            for j in range(2 * K // BLK):
                keep = jnp.where(lane == j, pattern[0, 0, level, i, j].astype(F32), keep)
            block = factors[level, i * BLK:(i + 1) * BLK, :].astype(F32) * keep
            masked[level, pl.ds(at + i * BLK, BLK), :] = block.astype(BF16)

    piece = jnp.zeros((K, K), F32)
    for c in range(CHUNKS):
        for copy in big[c]:
            copy.wait()
        cols = slice(c * width, (c + 1) * width)
        piece = piece + product(leaf[:, cols], omega[:, cols], ((1,), (1,)))
    half = K // 2
    at = pl.multiple_of(me * half, half)
    piece = piece.astype(BF16)
    gathered[0, pl.ds(at, half), :] = jnp.concatenate([piece[:half], piece[half:]], axis=1)
    pl.semaphore_wait(barrier, len(peers))
    pcopies = []
    for step, other in peers:
        copy = pltpu.make_async_remote_copy(
            src_ref=gathered.at[0, pl.ds(at, half), :],
            dst_ref=gathered.at[other, pl.ds(at, half), :],
            send_sem=psend.at[other, step], recv_sem=precv.at[other, step],
            device_id=peer(step, other), device_id_type=MESH,
        )
        copy.start()
        pcopies.append(copy)
    fcopies = [[], []]
    for level in range(LEVELS):
        at = pl.multiple_of(level_slot(level, me) * K, K)
        rows = masked.at[level, pl.ds(at, K), :]
        for step in (3, 1, 2):
            copy = pltpu.make_async_remote_copy(
                src_ref=rows, dst_ref=rows,
                send_sem=fsend.at[level, step], recv_sem=frecv.at[level, step],
                device_id=peer(step, 0), device_id_type=MESH,
            )
            copy.start()
            fcopies[level].append(copy)

    for copy in pcopies:
        copy.wait_recv()

    row = lax.broadcasted_iota(jnp.int32, (K, 1), 0)
    stacks = []
    for h in range(2):
        blocks = []
        for source in (2 * h, 2 * h + 1):
            mine, theirs = (gathered[o, source * half:(source + 1) * half, :] for o in (0, 1))
            blocks += [
                jnp.concatenate([mine[:, :K], theirs[:, :K]], axis=1),
                jnp.concatenate([mine[:, K:], theirs[:, K:]], axis=1),
            ]
        stacks.append(jnp.concatenate(blocks, axis=0))
    for level in range(LEVELS):
        for copy in fcopies[level]:
            copy.wait_recv()
        fresh = []
        for h in range(2):
            both = product(masked[level, h * 2 * K:(h + 1) * 2 * K, :], stacks[h]).astype(BF16)
            fresh += [both[:K], both[K:]]
        pieces = whiten(fresh, level == LEVELS - 1)
        pieces = [jnp.where(row < ranks[level], x, 0.0).astype(BF16) for x in pieces]
        if level == 0:
            stacks = [
                jnp.concatenate([pieces[0], pieces[2]], axis=0),
                jnp.concatenate([pieces[1], pieces[3]], axis=0),
            ]
    total = (pieces[0].astype(F32) + pieces[1].astype(F32)) + (
        pieces[2].astype(F32) + pieces[3].astype(F32)
    )
    load_outer.wait()
    if finish:
        out_ref[...] = product(total, outer[...], ((0,), (0,)))
    else:
        out_ref[...] = total
    for copy in fcopies[0] + fcopies[1]:
        copy.wait_send()
    for copy in pcopies:
        copy.wait_send()


def shards(omega, leaf, factors, pattern, ranks, outer):
    groups = lax.axis_size("src") // GROUP
    finish = groups == 1
    shape = (K, outer.shape[1]) if finish else (K, K)
    hbm = pl.BlockSpec(memory_space=pl.ANY)
    result = pl.pallas_call(
        lambda *refs: kernel(*refs, finish=finish),
        out_shape=jax.ShapeDtypeStruct(shape, F32),
        in_specs=[hbm] * 6,
        out_specs=pl.BlockSpec(memory_space=pltpu.VMEM),
        scratch_shapes=[
            pltpu.VMEM(omega.shape, BF16),
            pltpu.VMEM(leaf.shape[1:], BF16),
            pltpu.VMEM((LEVELS, K, 2 * K), BF16),
            pltpu.SMEM(pattern.shape, jnp.int32),
            pltpu.SMEM((LEVELS,), jnp.int32),
            pltpu.VMEM(outer.shape, BF16),
            pltpu.VMEM((LEVELS, GROUP * K, 2 * K), BF16),
            pltpu.VMEM((2, GROUP * K // 2, 2 * K), BF16),
            pltpu.SemaphoreType.DMA((4,)),
            pltpu.SemaphoreType.DMA((2, CHUNKS)),
            pltpu.SemaphoreType.DMA((LEVELS, GROUP)),
            pltpu.SemaphoreType.DMA((LEVELS, GROUP)),
            pltpu.SemaphoreType.DMA((2, GROUP)),
            pltpu.SemaphoreType.DMA((2, GROUP)),
        ],
        compiler_params=pltpu.CompilerParams(
            collective_id=0, has_side_effects=True
        ),
        cost_estimate=pl.CostEstimate(
            flops=2 * K * K * omega.shape[1], bytes_accessed=2 * omega.size * 2, transcendentals=0
        ),
    )(omega, leaf, factors, pattern, ranks, outer)
    if finish:
        return result
    total = lax.psum(result, "src") * (1.0 / GROUP)
    return lax.dot_general(
        total, outer.astype(F32), (((0,), (0,)), ((), ())), precision=lax.Precision.HIGHEST
    )


def solution(mesh):
    return jax.shard_map(
        shards,
        mesh=mesh,
        in_specs=(
            P("rep", "src"),
            P("tgt", None, "src"),
            P("tgt", "src", None, None, None),
            P("tgt", "src", None, None, None),
            P(),
            P(None, ("tgt", "src")),
        ),
        out_specs=P("rep", ("tgt", "src")),
        check_vma=False,
    )
```

```python
import jax
import jax.numpy as jnp
from jax import lax
from jax.experimental import pallas as pl
from jax.experimental.pallas import tpu as pltpu
from jax.sharding import PartitionSpec as P

K = 64
R_ALL = 128
BLK = 32
LEVELS = 2
GROUP = 4
CHUNKS = 4
MESH = pl.DeviceIdType.MESH

F32 = jnp.float32
BF16 = jnp.bfloat16


def product(left, right, dims=((1,), (0,))):
    return lax.dot_general(
        left.astype(BF16), right.astype(BF16), (dims, ((), ())), preferred_element_type=F32
    )


def level_slot(level, source):
    if level == 0:
        return source
    return source // 2 + 2 * (source % 2)


def whiten(fresh_bf, own):
    eye = (
        lax.broadcasted_iota(jnp.int32, (K, K), 0) == lax.broadcasted_iota(jnp.int32, (K, K), 1)
    ).astype(F32)
    count = len(fresh_bf)
    each = range(count)
    gram = [product(f, f, ((1,), (1,))) for f in fresh_bf]
    squared = [product(g, g) for g in gram]
    norm = [jnp.sum(jnp.sum(g * g, axis=1, keepdims=True), axis=0, keepdims=True) for g in gram]
    scale = [jnp.sqrt(n) + 1e-06 for n in norm]
    inv = [1.0 / s for s in scale]
    gain = [jnp.sqrt(R_ALL * i) for i in inv]
    a = [g * i for g, i in zip(gram, inv)]
    t = [s * i * i for s, i in zip(squared, inv)]
    target = [f[:, :K] if own else f for f in fresh_bf]
    w = [1.5 * target[i].astype(F32) - 0.5 * product(a[i], target[i]) for i in each]
    p = [2.25 * a[i] - 1.5 * t[i] + 0.25 * product(t[i], a[i]) for i in each]
    q = [product(p[i], p[i]) for i in each]
    w = [1.5 * w[i] - 0.5 * product(p[i], w[i]) for i in each]
    p = [2.25 * p[i] - 1.5 * q[i] + 0.25 * product(q[i], p[i]) for i in each]
    w = [1.5 * w[i] - 0.5 * product(p[i], w[i]) for i in each]
    return [w[i] * gain[i] for i in each]


def kernel(
    omega_hbm, leaf_hbm, factors_hbm, pattern_hbm, ranks_hbm, outer_hbm, out_ref,
    omega, leaf, factors, pattern, ranks, outer, masked, gathered,
    load_sem, chunk_sem, fsend, frecv, psend, precv, *, finish,
):
    src = lax.axis_index("src")
    tgt = lax.axis_index("tgt")
    rep = lax.axis_index("rep")
    base = src - lax.rem(src, GROUP)
    me = src - base

    def peer(step, other):
        high = lax.rem(me // 2 + step // 2, 2)
        low = lax.rem(lax.rem(me, 2) + step % 2, 2)
        return (base + 2 * high + low, tgt, lax.rem(rep + other, 2))

    peers = [(3, 0), (3, 1), (1, 0), (2, 0), (1, 1), (2, 1), (0, 1)]
    barrier = pltpu.get_barrier_semaphore()
    for step, other in peers:
        pl.semaphore_signal(barrier, inc=1, device_id=peer(step, other), device_id_type=MESH)

    small = [
        pltpu.make_async_copy(a, b, load_sem.at[i])
        for i, (a, b) in enumerate(
            (
                (pattern_hbm, pattern),
                (factors_hbm.at[0, 0], factors),
                (ranks_hbm, ranks),
            )
        )
    ]
    load_outer = pltpu.make_async_copy(outer_hbm, outer, load_sem.at[3])
    for copy in small:
        copy.start()
    width = omega.shape[1] // CHUNKS
    big = []
    for c in range(CHUNKS):
        cols = pl.ds(c * width, width)
        pair = (
            pltpu.make_async_copy(omega_hbm.at[:, cols], omega.at[:, cols], chunk_sem.at[0, c]),
            pltpu.make_async_copy(leaf_hbm.at[0, :, cols], leaf.at[:, cols], chunk_sem.at[1, c]),
        )
        for copy in pair:
            copy.start()
        big.append(pair)
    load_outer.start()

    for copy in small:
        copy.wait()
    lane = lax.broadcasted_iota(jnp.int32, (1, 2 * K), 1) // BLK
    for level in range(LEVELS):
        at = pl.multiple_of(level_slot(level, me) * K, K)
        for i in range(K // BLK):
            keep = jnp.zeros((1, 2 * K), F32)
            for j in range(2 * K // BLK):
                keep = jnp.where(lane == j, pattern[0, 0, level, i, j].astype(F32), keep)
            block = factors[level, i * BLK:(i + 1) * BLK, :].astype(F32) * keep
            masked[level, pl.ds(at + i * BLK, BLK), :] = block.astype(BF16)

    piece = jnp.zeros((K, K), F32)
    for c in range(CHUNKS):
        for copy in big[c]:
            copy.wait()
        cols = slice(c * width, (c + 1) * width)
        piece = piece + product(leaf[:, cols], omega[:, cols], ((1,), (1,)))
    half = K // 2
    at = pl.multiple_of(me * half, half)
    piece = piece.astype(BF16)
    gathered[0, pl.ds(at, half), :] = jnp.concatenate([piece[:half], piece[half:]], axis=1)
    pl.semaphore_wait(barrier, len(peers))
    pcopies = []
    for step, other in peers:
        copy = pltpu.make_async_remote_copy(
            src_ref=gathered.at[0, pl.ds(at, half), :],
            dst_ref=gathered.at[other, pl.ds(at, half), :],
            send_sem=psend.at[other, step], recv_sem=precv.at[other, step],
            device_id=peer(step, other), device_id_type=MESH,
        )
        copy.start()
        pcopies.append(copy)
    fcopies = [[], []]
    for level in range(LEVELS):
        at = pl.multiple_of(level_slot(level, me) * K, K)
        rows = masked.at[level, pl.ds(at, K), :]
        for step in (3, 1, 2):
            copy = pltpu.make_async_remote_copy(
                src_ref=rows, dst_ref=rows,
                send_sem=fsend.at[level, step], recv_sem=frecv.at[level, step],
                device_id=peer(step, 0), device_id_type=MESH,
            )
            copy.start()
            fcopies[level].append(copy)

    for copy in pcopies:
        copy.wait_recv()

    row = lax.broadcasted_iota(jnp.int32, (K, 1), 0)
    stacks = []
    for h in range(2):
        blocks = []
        for source in (2 * h, 2 * h + 1):
            mine, theirs = (gathered[o, source * half:(source + 1) * half, :] for o in (0, 1))
            blocks += [
                jnp.concatenate([mine[:, :K], theirs[:, :K]], axis=1),
                jnp.concatenate([mine[:, K:], theirs[:, K:]], axis=1),
            ]
        stacks.append(jnp.concatenate(blocks, axis=0))
    for level in range(LEVELS):
        for copy in fcopies[level]:
            copy.wait_recv()
        fresh = []
        for h in range(2):
            both = product(masked[level, h * 2 * K:(h + 1) * 2 * K, :], stacks[h]).astype(BF16)
            fresh += [both[:K], both[K:]]
        pieces = whiten(fresh, level == LEVELS - 1)
        pieces = [jnp.where(row < ranks[level], x, 0.0).astype(BF16) for x in pieces]
        if level == 0:
            stacks = [
                jnp.concatenate([pieces[0], pieces[2]], axis=0),
                jnp.concatenate([pieces[1], pieces[3]], axis=0),
            ]
    total = (pieces[0].astype(F32) + pieces[1].astype(F32)) + (
        pieces[2].astype(F32) + pieces[3].astype(F32)
    )
    load_outer.wait()
    if finish:
        out_ref[...] = product(total, outer[...], ((0,), (0,)))
    else:
        out_ref[...] = total
    for copy in fcopies[0] + fcopies[1]:
        copy.wait_send()
    for copy in pcopies:
        copy.wait_send()


def shards(omega, leaf, factors, pattern, ranks, outer):
    groups = lax.axis_size("src") // GROUP
    finish = groups == 1
    shape = (K, outer.shape[1]) if finish else (K, K)
    hbm = pl.BlockSpec(memory_space=pl.ANY)
    result = pl.pallas_call(
        lambda *refs: kernel(*refs, finish=finish),
        out_shape=jax.ShapeDtypeStruct(shape, F32),
        in_specs=[hbm] * 6,
        out_specs=pl.BlockSpec(memory_space=pltpu.VMEM),
        scratch_shapes=[
            pltpu.VMEM(omega.shape, BF16),
            pltpu.VMEM(leaf.shape[1:], BF16),
            pltpu.VMEM((LEVELS, K, 2 * K), BF16),
            pltpu.SMEM(pattern.shape, jnp.int32),
            pltpu.SMEM((LEVELS,), jnp.int32),
            pltpu.VMEM(outer.shape, BF16),
            pltpu.VMEM((LEVELS, GROUP * K, 2 * K), BF16),
            pltpu.VMEM((2, GROUP * K // 2, 2 * K), BF16),
            pltpu.SemaphoreType.DMA((4,)),
            pltpu.SemaphoreType.DMA((2, CHUNKS)),
            pltpu.SemaphoreType.DMA((LEVELS, GROUP)),
            pltpu.SemaphoreType.DMA((LEVELS, GROUP)),
            pltpu.SemaphoreType.DMA((2, GROUP)),
            pltpu.SemaphoreType.DMA((2, GROUP)),
        ],
        compiler_params=pltpu.CompilerParams(
            collective_id=0, has_side_effects=True, vmem_limit_bytes=32 * 1024 * 1024
        ),
        cost_estimate=pl.CostEstimate(
            flops=2 * K * K * omega.shape[1], bytes_accessed=2 * omega.size * 2, transcendentals=0
        ),
    )(*(pltpu.with_memory_space_constraint(x, pltpu.HBM)
        for x in (omega, leaf, factors, pattern, ranks, outer)))
    if finish:
        return result
    total = lax.psum(result, "src") * (1.0 / GROUP)
    return lax.dot_general(
        total, outer.astype(F32), (((0,), (0,)), ((), ())), precision=lax.Precision.HIGHEST
    )


def solution(mesh):
    return jax.shard_map(
        shards,
        mesh=mesh,
        in_specs=(
            P("rep", "src"),
            P("tgt", None, "src"),
            P("tgt", "src", None, None, None),
            P("tgt", "src", None, None, None),
            P(),
            P(None, ("tgt", "src")),
        ),
        out_specs=P("rep", ("tgt", "src")),
        check_vma=False,
    )
```

```python
import jax
import jax.numpy as jnp
from jax import lax
from jax.experimental import pallas as pl
from jax.experimental.pallas import tpu as pltpu
from jax.sharding import PartitionSpec as P

K = 64
R_ALL = 128
BLK = 32
LEVELS = 2
GROUP = 4
CHUNKS = 4
MESH = pl.DeviceIdType.MESH

F32 = jnp.float32
BF16 = jnp.bfloat16


def product(left, right, dims=((1,), (0,))):
    return lax.dot_general(
        left.astype(BF16), right.astype(BF16), (dims, ((), ())), preferred_element_type=F32
    )


def level_slot(level, source):
    if level == 0:
        return source
    return source // 2 + 2 * (source % 2)


def whiten(fresh_bf, own):
    eye = (
        lax.broadcasted_iota(jnp.int32, (K, K), 0) == lax.broadcasted_iota(jnp.int32, (K, K), 1)
    ).astype(F32)
    count = len(fresh_bf)
    each = range(count)
    gram = [product(f, f, ((1,), (1,))) for f in fresh_bf]
    squared = [product(g, g) for g in gram]
    norm = [jnp.sum(jnp.sum(g * g, axis=1, keepdims=True), axis=0, keepdims=True) for g in gram]
    scale = [jnp.sqrt(n) + 1e-06 for n in norm]
    inv = [1.0 / s for s in scale]
    gain = [jnp.sqrt(R_ALL * i) for i in inv]
    a = [g * i for g, i in zip(gram, inv)]
    t = [s * i * i for s, i in zip(squared, inv)]
    target = [f[:, :K] if own else f for f in fresh_bf]
    w = [1.5 * target[i].astype(F32) - 0.5 * product(a[i], target[i]) for i in each]
    p = [2.25 * a[i] - 1.5 * t[i] + 0.25 * product(t[i], a[i]) for i in each]
    q = [product(p[i], p[i]) for i in each]
    w = [1.5 * w[i] - 0.5 * product(p[i], w[i]) for i in each]
    p = [2.25 * p[i] - 1.5 * q[i] + 0.25 * product(q[i], p[i]) for i in each]
    w = [1.5 * w[i] - 0.5 * product(p[i], w[i]) for i in each]
    return [w[i] * gain[i] for i in each]


def kernel(
    omega_hbm, leaf_hbm, factors_hbm, pattern_hbm, ranks_hbm, outer_hbm, out_ref,
    omega, leaf, factors, pattern, ranks, outer, masked, gathered,
    load_sem, chunk_sem, fsend, frecv, psend, precv, *, finish,
):
    src = lax.axis_index("src")
    tgt = lax.axis_index("tgt")
    rep = lax.axis_index("rep")
    base = src - lax.rem(src, GROUP)
    me = src - base

    def peer(step, other):
        high = lax.rem(me // 2 + step // 2, 2)
        low = lax.rem(lax.rem(me, 2) + step % 2, 2)
        return (base + 2 * high + low, tgt, lax.rem(rep + other, 2))

    peers = [(3, 0), (3, 1), (1, 0), (2, 0), (1, 1), (2, 1), (0, 1)]
    barrier = pltpu.get_barrier_semaphore()
    for step, other in peers:
        pl.semaphore_signal(barrier, inc=1, device_id=peer(step, other), device_id_type=MESH)

    small = [
        pltpu.make_async_copy(a, b, load_sem.at[i])
        for i, (a, b) in enumerate(
            (
                (pattern_hbm, pattern),
                (factors_hbm.at[0, 0], factors),
                (ranks_hbm, ranks),
            )
        )
    ]
    load_outer = pltpu.make_async_copy(outer_hbm, outer, load_sem.at[3])
    for copy in small:
        copy.start()
    width = omega.shape[1] // CHUNKS
    big = []
    for c in range(CHUNKS):
        cols = pl.ds(c * width, width)
        pair = (
            pltpu.make_async_copy(omega_hbm.at[:, cols], omega.at[:, cols], chunk_sem.at[0, c]),
            pltpu.make_async_copy(leaf_hbm.at[0, :, cols], leaf.at[:, cols], chunk_sem.at[1, c]),
        )
        for copy in pair:
            copy.start()
        big.append(pair)
    load_outer.start()

    for copy in small:
        copy.wait()
    lane = lax.broadcasted_iota(jnp.int32, (1, 2 * K), 1) // BLK
    for level in range(LEVELS):
        at = pl.multiple_of(level_slot(level, me) * K, K)
        for i in range(K // BLK):
            keep = jnp.zeros((1, 2 * K), F32)
            for j in range(2 * K // BLK):
                keep = jnp.where(lane == j, pattern[0, 0, level, i, j].astype(F32), keep)
            block = factors[level, i * BLK:(i + 1) * BLK, :].astype(F32) * keep
            masked[level, pl.ds(at + i * BLK, BLK), :] = block.astype(BF16)

    piece = jnp.zeros((K, K), F32)
    for c in range(CHUNKS):
        for copy in big[c]:
            copy.wait()
        cols = slice(c * width, (c + 1) * width)
        piece = piece + product(leaf[:, cols], omega[:, cols], ((1,), (1,)))
    half = K // 2
    at = pl.multiple_of(me * half, half)
    piece = piece.astype(BF16)
    gathered[0, pl.ds(at, half), :] = jnp.concatenate([piece[:half], piece[half:]], axis=1)
    pl.semaphore_wait(barrier, len(peers))
    pcopies = []
    fcopies = [[], []]

    def send_piece(step, other):
        copy = pltpu.make_async_remote_copy(
            src_ref=gathered.at[0, pl.ds(at, half), :],
            dst_ref=gathered.at[other, pl.ds(at, half), :],
            send_sem=psend.at[other, step], recv_sem=precv.at[other, step],
            device_id=peer(step, other), device_id_type=MESH,
        )
        copy.start()
        pcopies.append(copy)

    def send_factor(step, level):
        rows = masked.at[level, pl.ds(pl.multiple_of(level_slot(level, me) * K, K), K), :]
        copy = pltpu.make_async_remote_copy(
            src_ref=rows, dst_ref=rows,
            send_sem=fsend.at[level, step], recv_sem=frecv.at[level, step],
            device_id=peer(step, 0), device_id_type=MESH,
        )
        copy.start()
        fcopies[level].append(copy)

    for step in (3, 1, 2):
        send_factor(step, 0)
        send_piece(step, 0)
        send_piece(step, 1)
    send_piece(0, 1)
    for step in (3, 1, 2):
        send_factor(step, 1)
    for copy in pcopies:
        copy.wait_recv()

    row = lax.broadcasted_iota(jnp.int32, (K, 1), 0)
    stacks = []
    for h in range(2):
        blocks = []
        for source in (2 * h, 2 * h + 1):
            mine, theirs = (gathered[o, source * half:(source + 1) * half, :] for o in (0, 1))
            blocks += [
                jnp.concatenate([mine[:, :K], theirs[:, :K]], axis=1),
                jnp.concatenate([mine[:, K:], theirs[:, K:]], axis=1),
            ]
        stacks.append(jnp.concatenate(blocks, axis=0))
    for level in range(LEVELS):
        for copy in fcopies[level]:
            copy.wait_recv()
        fresh = []
        for h in range(2):
            both = product(masked[level, h * 2 * K:(h + 1) * 2 * K, :], stacks[h]).astype(BF16)
            fresh += [both[:K], both[K:]]
        pieces = whiten(fresh, level == LEVELS - 1)
        pieces = [jnp.where(row < ranks[level], x, 0.0).astype(BF16) for x in pieces]
        if level == 0:
            stacks = [
                jnp.concatenate([pieces[0], pieces[2]], axis=0),
                jnp.concatenate([pieces[1], pieces[3]], axis=0),
            ]
    total = (pieces[0].astype(F32) + pieces[1].astype(F32)) + (
        pieces[2].astype(F32) + pieces[3].astype(F32)
    )
    load_outer.wait()
    if finish:
        out_ref[...] = product(total, outer[...], ((0,), (0,)))
    else:
        out_ref[...] = total
    for copy in fcopies[0] + fcopies[1]:
        copy.wait_send()
    for copy in pcopies:
        copy.wait_send()


def shards(omega, leaf, factors, pattern, ranks, outer):
    groups = lax.axis_size("src") // GROUP
    finish = groups == 1
    shape = (K, outer.shape[1]) if finish else (K, K)
    hbm = pl.BlockSpec(memory_space=pl.ANY)
    result = pl.pallas_call(
        lambda *refs: kernel(*refs, finish=finish),
        out_shape=jax.ShapeDtypeStruct(shape, F32),
        in_specs=[hbm] * 6,
        out_specs=pl.BlockSpec(memory_space=pltpu.VMEM),
        scratch_shapes=[
            pltpu.VMEM(omega.shape, BF16),
            pltpu.VMEM(leaf.shape[1:], BF16),
            pltpu.VMEM((LEVELS, K, 2 * K), BF16),
            pltpu.SMEM(pattern.shape, jnp.int32),
            pltpu.SMEM((LEVELS,), jnp.int32),
            pltpu.VMEM(outer.shape, BF16),
            pltpu.VMEM((LEVELS, GROUP * K, 2 * K), BF16),
            pltpu.VMEM((2, GROUP * K // 2, 2 * K), BF16),
            pltpu.SemaphoreType.DMA((4,)),
            pltpu.SemaphoreType.DMA((2, CHUNKS)),
            pltpu.SemaphoreType.DMA((LEVELS, GROUP)),
            pltpu.SemaphoreType.DMA((LEVELS, GROUP)),
            pltpu.SemaphoreType.DMA((2, GROUP)),
            pltpu.SemaphoreType.DMA((2, GROUP)),
        ],
        compiler_params=pltpu.CompilerParams(
            collective_id=0, has_side_effects=True, vmem_limit_bytes=32 * 1024 * 1024
        ),
        cost_estimate=pl.CostEstimate(
            flops=2 * K * K * omega.shape[1], bytes_accessed=2 * omega.size * 2, transcendentals=0
        ),
    )(*(pltpu.with_memory_space_constraint(x, pltpu.HBM)
        for x in (omega, leaf, factors, pattern, ranks, outer)))
    if finish:
        return result
    total = lax.psum(result, "src") * (1.0 / GROUP)
    return lax.dot_general(
        total, outer.astype(F32), (((0,), (0,)), ((), ())), precision=lax.Precision.HIGHEST
    )


def solution(mesh):
    return jax.shard_map(
        shards,
        mesh=mesh,
        in_specs=(
            P("rep", "src"),
            P("tgt", None, "src"),
            P("tgt", "src", None, None, None),
            P("tgt", "src", None, None, None),
            P(),
            P(None, ("tgt", "src")),
        ),
        out_specs=P("rep", ("tgt", "src")),
        check_vma=False,
    )
```
